128 devices in a mesh: outer: 2 (over core), inner: 16 (over z, y), head: 4 (over x).
Axes of the slice: x: 4, y: 4, z: 4, core: 2. Of those that a mesh axis runs over, the one named last changes fastest.
Arguments:
- queries: bfloat16 [4096, 8192], P(('outer', 'inner'), 'head'), may hold values from -5.5 to 5.5
- keys: bfloat16 [4096, 1024], P(('outer', 'inner'), 'head'), may hold values from -5.5 to 5.5
- values: bfloat16 [4096, 1024], P(('outer', 'inner'), 'head'), may hold values from -6 to 6
- output_cotangent: bfloat16 [4096, 8192], P(('outer', 'inner'), 'head'), may hold values from -6 to 6
- positions: int32 [4096], P(('outer', 'inner')), may hold values from 0 to 4095, as said below
Outputs:
- attn_out: bfloat16 [4096, 8192], P(('outer', 'inner'), 'head')
- grad_queries: bfloat16 [4096, 8192], P(('outer', 'inner'), 'head')
- key_gradient: bfloat16 [4096, 1024], P(('outer', 'inner'), 'head')
- value_gradient: bfloat16 [4096, 1024], P(('outer', 'inner'), 'head')
The draws below stay inside these ranges and needn't reach their ends.
Inputs may be any that keep to these rules, and one draw needn't show every extreme that they name: The 128 positions of each index of outer+inner are two runs of 64 consecutive ascending positions, each starting at a multiple of 64; all 4096 together are a permutation.
All inputs are finite; a program needn't handle non-finite values.
Results may differ from the reference program's by a relative error of at most 0.039.
Values may be sent and summed in bfloat16 or wider, within the bound.
No kernel may reach another device: no remote copies, remote signals or barrier semaphores. Data moves between devices by JAX's collectives and lax.ppermute only.
A program may use at most 64 MiB of HBM per device.

```python
import math
import jax
import jax.numpy as jnp
from jax import lax

QUERY_HEADS = 64
KEY_VALUE_HEADS = 8
HEAD_SIZE = 128
TOK_DEV = 128
SEQUENCE_TOKENS = 4096


def block_order(key):
    return jax.random.permutation(jax.random.fold_in(key, 11), SEQUENCE_TOKENS // (TOK_DEV // 2))


def draw_positions(key, part):
    order = block_order(key)
    half_rows = TOK_DEV // 2
    table = order[:, None] * half_rows + jnp.arange(half_rows, dtype=jnp.int32)[None, :]
    return table.reshape(SEQUENCE_TOKENS).astype(jnp.int32)


def draw_queries(key, part):
    key = jax.random.fold_in(key, 3)
    return jnp.clip(jax.random.normal(key, (SEQUENCE_TOKENS, QUERY_HEADS * HEAD_SIZE), jnp.float32), -4.0, 4.0).astype(jnp.bfloat16)


def draw_keys(key, part):
    key = jax.random.fold_in(key, 5)
    return jnp.clip(jax.random.normal(key, (SEQUENCE_TOKENS, KEY_VALUE_HEADS * HEAD_SIZE), jnp.float32), -4.0, 4.0).astype(jnp.bfloat16)


def steps_of(own_key, shape, split, smallest, largest):
    loudness = 1.0
    for axis_at, parts in split:
        heights = jax.random.uniform(jax.random.fold_in(jax.random.fold_in(own_key, 6), axis_at), (parts,), jnp.float32, smallest / len(split), largest / len(split))
        loudness = loudness * jnp.repeat(jnp.exp(heights), shape[axis_at] // parts).reshape((-1,) + (1,) * (len(shape) - 1 - axis_at))
    return loudness


def bell_draw(rng, extent, deviation, most, cuts=(), kind=jnp.bfloat16):
    result = jax.random.normal(rng, extent, jnp.float32) * deviation
    if len(cuts) > 0:
        result = steps_of(rng, extent, cuts, -0.22, 0.18) * result
    return jnp.clip(result, min=-most, max=most).astype(kind)


def setup_inputs(seed: int = 0) -> dict:
    streams_of = jax.random.split(jax.random.key(seed), 6)
    queries = draw_queries(jax.random.fold_in(streams_of[5], 71), 0)
    keys = draw_keys(jax.random.fold_in(streams_of[5], 71), 0)
    values = bell_draw(streams_of[2], (SEQUENCE_TOKENS, KEY_VALUE_HEADS * HEAD_SIZE), 1.0, 6.0, ((0, 32), (1, 4)))
    output_cotangent = bell_draw(streams_of[3], (SEQUENCE_TOKENS, QUERY_HEADS * HEAD_SIZE), 1.0, 6.0, ((0, 32), (1, 4)))
    positions = draw_positions(jax.random.fold_in(streams_of[5], 71), 0)
    return {"queries": queries, "keys": keys, "values": values, "output_cotangent": output_cotangent, "positions": positions}


NEG_FILL = -1e30


def rounded(tensor):
    return lax.optimization_barrier(tensor.astype(jnp.bfloat16)).astype(jnp.float32)


def reference(queries, keys, values, output_cotangent, positions):
    group_repeat = QUERY_HEADS // KEY_VALUE_HEADS
    score_scale = HEAD_SIZE ** -0.5
    block_rows = math.gcd(SEQUENCE_TOKENS, 512)
    query_heads = queries.reshape(SEQUENCE_TOKENS, KEY_VALUE_HEADS, group_repeat, HEAD_SIZE).transpose(1, 0, 2, 3)
    output_grad_heads = output_cotangent.reshape(SEQUENCE_TOKENS, KEY_VALUE_HEADS, group_repeat, HEAD_SIZE).transpose(1, 0, 2, 3)
    key_heads = keys.reshape(SEQUENCE_TOKENS, KEY_VALUE_HEADS, HEAD_SIZE).transpose(1, 0, 2)
    value_heads = values.reshape(SEQUENCE_TOKENS, KEY_VALUE_HEADS, HEAD_SIZE).transpose(1, 0, 2)
    highest = lax.Precision.HIGHEST

    def one_group(operands):
        q_group, do_group, k_group, v_group = operands
        k_full = k_group.astype(jnp.float32)
        v_full = v_group.astype(jnp.float32)

        def walk_block(sums_carry, block_index):
            grad_k, grad_v = sums_carry
            first_row = block_index * block_rows
            q_blk = lax.dynamic_slice_in_dim(q_group, first_row, block_rows, 0).astype(jnp.float32)
            do_blk = lax.dynamic_slice_in_dim(do_group, first_row, block_rows, 0).astype(jnp.float32)
            pos_blk = lax.dynamic_slice_in_dim(positions, first_row, block_rows, 0)
            allowed = positions[None, None, :] <= pos_blk[None, :, None]
            scores = jnp.einsum('nrd,md->rnm', q_blk, k_full, precision=highest) * score_scale
            scores = jnp.where(allowed, scores, NEG_FILL)
            row_max = jnp.max(scores, axis=-1)
            weights = jnp.where(allowed, jnp.exp(scores - row_max[..., None]), 0.0)
            row_total = jnp.sum(weights, axis=-1)
            mixed_rows = jnp.einsum('rnm,md->nrd', rounded(weights), v_full, precision=highest)
            out_blk = (mixed_rows / jnp.transpose(row_total)[:, :, None]).astype(jnp.bfloat16)
            log_total = row_max + jnp.log(row_total)
            row_delta = jnp.transpose(jnp.sum(do_blk * out_blk.astype(jnp.float32), axis=-1))
            probabilities = jnp.where(allowed, jnp.exp(scores - log_total[..., None]), 0.0)
            grad_v = grad_v + jnp.einsum('rnm,nrd->md', rounded(probabilities), do_blk, precision=highest)
            grad_probs = jnp.einsum('nrd,md->rnm', do_blk, v_full, precision=highest)
            dscore = rounded(probabilities * (grad_probs - row_delta[..., None]) * score_scale)
            grad_q = jnp.einsum('rnm,md->nrd', dscore, k_full, precision=highest).astype(jnp.bfloat16)
            grad_k = grad_k + jnp.einsum('rnm,nrd->md', dscore, q_blk, precision=highest)
            return (grad_k, grad_v), (out_blk, grad_q)

        zero_rows = jnp.zeros((SEQUENCE_TOKENS, HEAD_SIZE), jnp.float32)
        block_ids = jnp.arange(SEQUENCE_TOKENS // block_rows, dtype=jnp.int32)
        (grad_k, grad_v), (out_blocks, grad_blocks) = lax.scan(walk_block, (zero_rows, zero_rows), block_ids)
        return (out_blocks.reshape(SEQUENCE_TOKENS, group_repeat, HEAD_SIZE), grad_blocks.reshape(SEQUENCE_TOKENS, group_repeat, HEAD_SIZE),
                grad_k.astype(jnp.bfloat16), grad_v.astype(jnp.bfloat16))

    out_all, grad_q_all, key_gradient_total, value_gradient_total = lax.map(one_group, (query_heads, output_grad_heads, key_heads, value_heads))
    attn_out = out_all.transpose(1, 0, 2, 3).reshape(SEQUENCE_TOKENS, QUERY_HEADS * HEAD_SIZE)
    grad_queries = grad_q_all.transpose(1, 0, 2, 3).reshape(SEQUENCE_TOKENS, QUERY_HEADS * HEAD_SIZE)
    key_gradient = key_gradient_total.transpose(1, 0, 2).reshape(SEQUENCE_TOKENS, KEY_VALUE_HEADS * HEAD_SIZE)
    value_gradient = value_gradient_total.transpose(1, 0, 2).reshape(SEQUENCE_TOKENS, KEY_VALUE_HEADS * HEAD_SIZE)
    return (attn_out, grad_queries, key_gradient, value_gradient)
```

```python
import functools
import math

import jax
import jax.numpy as jnp
from jax import lax
from jax.experimental import pallas as pl
from jax.experimental.pallas import tpu as pltpu
from jax.sharding import PartitionSpec as P

HEAD = 128
HEADS = 8
RUN = 64
ROWS = RUN * HEADS
TOK = 128
TAIL = 16
SIDE = 4
BLOCKS = 64
CHUNK = 1024
SCALE = HEAD**-0.5
SCALE2 = SCALE * math.log2(math.e)
NEG = -1e30

bf16 = jnp.bfloat16
f32 = jnp.float32


def dot(a, b):
    return lax.dot_general(a, b, (((1,), (0,)), ((), ())), preferred_element_type=f32)


def attention_kernel(*refs):
    own_ref, q_ref, do_ref = refs[:3]
    kv_refs = refs[3:11]
    out_ref, gq_ref = refs[11:13]
    dkv_refs = refs[13:21]
    (ids_v, ids_s, sem, ka, va, kt, vt, qn, qt, don, dot_t, sbuf, wbuf, dka, dva) = refs[21:]
    tokens = BLOCKS * RUN
    step = TOK + TAIL
    lane = lax.broadcasted_iota(jnp.int32, (RUN, HEAD), 1)
    sub = lax.broadcasted_iota(jnp.int32, (RUN, HEAD), 0)
    diff = jnp.where(lane < RUN, sub - lane, -(1 << 30))

    for part in range(8):
        for unit in range(SIDE):
            tail = kv_refs[part][unit * step + TOK : (unit + 1) * step, 0:HEAD]
            row = part * SIDE + unit
            ids_v[row : row + 1, :] = tail.astype(f32)[0:1, :].astype(jnp.int32)
    fetch = pltpu.make_async_copy(ids_v, ids_s, sem)
    fetch.start()
    fetch.wait()

    for part in range(8):
        for unit in range(SIDE):
            for run in range(2):
                where = ids_s[part * SIDE + unit, run]
                place = pl.ds(pl.multiple_of(where * RUN, RUN), RUN)
                first = unit * step + run * RUN
                ka[place, 0:HEAD] = kv_refs[part][first : first + RUN, 0:HEAD]
                va[place, 0:HEAD] = kv_refs[part][first : first + RUN, HEAD : 2 * HEAD]
    ones3 = jnp.where(lax.broadcasted_iota(jnp.int32, (CHUNK, HEAD), 1) < 3, 1.0, 0.0).astype(bf16)
    ones1 = jnp.where(lax.broadcasted_iota(jnp.int32, (TAIL, CHUNK), 0) < 1, 1.0, 0.0).astype(bf16)

    @pl.loop(0, tokens // CHUNK)
    def _(c):
        s = pl.ds(pl.multiple_of(c * CHUNK, CHUNK), CHUNK)
        va[s, HEAD : 2 * HEAD] = ones3
        kt[:, s] = jnp.transpose(ka[s, 0:HEAD])
        vt[0:HEAD, s] = jnp.transpose(va[s, 0:HEAD])
        vt[HEAD : HEAD + TAIL, s] = ones1
        dka[s, :] = jnp.zeros((CHUNK, HEAD), f32)
        dva[s, :] = jnp.zeros((CHUNK, HEAD), f32)

    token_of = lax.broadcasted_iota(jnp.int32, (HEAD, ROWS), 1) & (RUN - 1)
    depth_of = lax.broadcasted_iota(jnp.int32, (HEAD, ROWS), 0)
    qt[HEAD : 2 * HEAD, :] = jnp.where(token_of == depth_of, 1.0, 0.0).astype(bf16)

    @pl.loop(0, 4)
    def _(a):
        position = own_ref[a]
        turns = position * RUN // CHUNK + 1
        rows = pl.ds(pl.multiple_of(a * RUN, RUN), RUN)
        for h in range(HEADS):
            qn[h * RUN : (h + 1) * RUN, :] = q_ref[rows, h * HEAD : (h + 1) * HEAD]
            don[h * RUN : (h + 1) * RUN, :] = do_ref[rows, h * HEAD : (h + 1) * HEAD]
        qt[0:HEAD, :] = jnp.transpose(qn[...])

        def score_turn(c, largest):
            base = pl.multiple_of(c * CHUNK, CHUNK)
            for j in range(CHUNK // RUN):
                limit = (position - c * (CHUNK // RUN) - j) * RUN
                place = pl.ds(pl.multiple_of(base + j * RUN, RUN), RUN)
                ka[place, HEAD : 2 * HEAD] = jnp.where(diff <= limit, 0.0, NEG).astype(bf16)
            scores = dot(ka[pl.ds(base, CHUNK), :], qt[...]) * SCALE2
            sbuf[pl.ds(base, CHUNK), :] = scores
            return jnp.maximum(largest, jnp.max(scores.reshape(CHUNK // 8, 8, ROWS), axis=0))

        largest = lax.fori_loop(0, turns, score_turn, jnp.full((8, ROWS), NEG, f32))
        row_max = jnp.max(largest, axis=0, keepdims=True)

        def weight_turn(c, mixed):
            s = pl.ds(pl.multiple_of(c * CHUNK, CHUNK), CHUNK)
            weights = jnp.exp2(sbuf[s, :] - row_max).astype(bf16)
            wbuf[s, :] = weights
            return mixed + dot(vt[:, s], weights)

        mixed = lax.fori_loop(0, turns, weight_turn, jnp.zeros((HEAD + TAIL, ROWS), f32))
        inverse = 1.0 / mixed[HEAD : HEAD + 1, :]
        out_t = (mixed[0:HEAD, :] * inverse).astype(bf16)
        out_n = jnp.transpose(out_t)
        do_t = (jnp.transpose(don[...]).astype(f32) * inverse).astype(bf16)
        don[...] = jnp.transpose(do_t)
        delta = -jnp.sum(do_t.astype(f32) * out_t.astype(f32), axis=0, keepdims=True)
        high = delta.astype(bf16).astype(f32)
        middle = (delta - high).astype(bf16).astype(f32)
        low = delta - high - middle
        dot_t[0:HEAD, :] = do_t
        dot_t[HEAD : 2 * HEAD, :] = jnp.where(
            depth_of == 0,
            high,
            jnp.where(depth_of == 1, middle, jnp.where(depth_of == 2, low, 0.0)),
        ).astype(bf16)
        for h in range(HEADS):
            out_ref[rows, h * HEAD : (h + 1) * HEAD] = out_n[h * RUN : (h + 1) * RUN, :]

        def gradient_turn(c, grad_q):
            s = pl.ds(pl.multiple_of(c * CHUNK, CHUNK), CHUNK)
            weights = wbuf[s, :]
            dscore = weights * dot(va[s, :], dot_t[...]).astype(bf16)
            dva[s, :] += dot(weights, don[...])
            dka[s, :] += dot(dscore, qn[...])
            return grad_q + dot(kt[:, s], dscore)

        grad_q = lax.fori_loop(0, turns, gradient_turn, jnp.zeros((HEAD, ROWS), f32))
        grad_n = jnp.transpose((grad_q * SCALE).astype(bf16))
        for h in range(HEADS):
            gq_ref[rows, h * HEAD : (h + 1) * HEAD] = grad_n[h * RUN : (h + 1) * RUN, :]

    for part in range(8):
        for unit in range(SIDE):
            for run in range(2):
                where = ids_s[part * SIDE + unit, run]
                place = pl.ds(pl.multiple_of(where * RUN, RUN), RUN)
                first = unit * TOK + run * RUN
                dkv_refs[part][first : first + RUN, 0:HEAD] = (dka[place, :] * SCALE).astype(bf16)
                dkv_refs[part][first : first + RUN, HEAD : 2 * HEAD] = dva[place, :].astype(bf16)


def attention(own, q, do, kv):
    vmem = pl.BlockSpec(memory_space=pltpu.VMEM)
    smem = pl.BlockSpec(memory_space=pltpu.SMEM)
    tokens = BLOCKS * RUN
    wide = jax.ShapeDtypeStruct(q.shape, bf16)
    part = jax.ShapeDtypeStruct((SIDE * TOK, 2 * HEAD), bf16)
    return pl.pallas_call(
        attention_kernel,
        out_shape=(wide, wide) + (part,) * 8,
        in_specs=[smem] + [vmem] * 10,
        out_specs=(vmem,) * 10,
        scratch_shapes=[
            pltpu.VMEM((32, HEAD), jnp.int32),
            pltpu.SMEM((32, HEAD), jnp.int32),
            pltpu.SemaphoreType.DMA,
            pltpu.VMEM((tokens, 2 * HEAD), bf16),
            pltpu.VMEM((tokens, 2 * HEAD), bf16),
            pltpu.VMEM((HEAD, tokens), bf16),
            pltpu.VMEM((HEAD + TAIL, tokens), bf16),
            pltpu.VMEM((ROWS, HEAD), bf16),
            pltpu.VMEM((2 * HEAD, ROWS), bf16),
            pltpu.VMEM((ROWS, HEAD), bf16),
            pltpu.VMEM((2 * HEAD, ROWS), bf16),
            pltpu.VMEM((tokens, ROWS), f32),
            pltpu.VMEM((tokens, ROWS), bf16),
            pltpu.VMEM((tokens, HEAD), f32),
            pltpu.VMEM((tokens, HEAD), f32),
        ],
        compiler_params=pltpu.CompilerParams(vmem_limit_bytes=56 * 2**20),
        name="attention",
    )(own, q, do, *kv)


def swap(x):
    return lax.ppermute(x, "outer", [(0, 1), (1, 0)])


def shift(x, dz, dy):
    pairs = [
        (z * SIDE + y, (z + dz) % SIDE * SIDE + (y + dy) % SIDE)
        for z in range(SIDE)
        for y in range(SIDE)
    ]
    return lax.ppermute(x, "inner", pairs)


def body(queries, keys, values, output_cotangent, positions):
    core = lax.axis_index("outer")

    def halves(x):
        width = x.shape[1] // 2
        first, second = x[:, :width], x[:, width:]
        mine = jnp.where(core == 0, first, second)
        other = jnp.where(core == 0, second, first)
        return mine, other

    keys_mine, keys_other = halves(keys)
    values_mine, values_other = halves(values)
    own_ids = positions.reshape(2, RUN)[:, 0] // RUN
    tail = jnp.zeros((TAIL, 2 * HEAD), bf16).at[0, 0:2].set(own_ids.astype(bf16))
    kv_mine = jnp.concatenate([jnp.concatenate([keys_mine, values_mine], 1), tail], 0)
    kv_other = swap(jnp.concatenate([jnp.concatenate([keys_other, values_other], 1), tail], 0))
    q_mine, q_other = halves(queries)
    do_mine, do_other = halves(output_cotangent)
    q_other = swap(q_other)
    do_other = swap(do_other)

    def along_y(x, d):
        return shift(x, 0, d)

    def along_z(x, d):
        return shift(x, d, 0)

    def gather(x, first, second):
        line = jnp.concatenate([x] + [first(x, d) for d in range(1, SIDE)], 0)
        return [line] + [second(line, d) for d in range(1, SIDE)]

    kv = gather(kv_mine, along_y, along_z) + gather(kv_other, along_z, along_y)
    q = jnp.concatenate([q_mine, q_other], 0)
    do = jnp.concatenate([do_mine, do_other], 0)
    partner_ids = kv_other[TOK, 0:2].astype(jnp.int32)
    own = jnp.concatenate([own_ids, partner_ids])

    results = attention(own, q, do, kv)
    out, grad_q = results[:2]
    parts = results[2:]

    def total(terms):
        return functools.reduce(jnp.add, [t.astype(f32) for t in terms]).astype(bf16)

    def scatter(lines, first, second):
        line = total([lines[0]] + [second(lines[d], -d) for d in range(1, SIDE)])
        units = [line[d * TOK : (d + 1) * TOK] for d in range(SIDE)]
        return total([units[0]] + [first(units[d], -d) for d in range(1, SIDE)])

    dkv_mine = scatter(parts[:4], along_y, along_z)
    dkv_other = swap(scatter(parts[4:], along_z, along_y))

    def join(mine, other):
        return jnp.where(
            core == 0, jnp.concatenate([mine, other], 1), jnp.concatenate([other, mine], 1)
        )

    attn_out = join(out[:TOK], swap(out[TOK:]))
    grad_queries = join(grad_q[:TOK], swap(grad_q[TOK:]))
    key_gradient = join(dkv_mine[:, :HEAD], dkv_other[:, :HEAD])
    value_gradient = join(dkv_mine[:, HEAD:], dkv_other[:, HEAD:])
    return attn_out, grad_queries, key_gradient, value_gradient


def solution(mesh):
    tokens = ("outer", "inner")
    split = P(tokens, "head")
    return jax.shard_map(
        body,
        mesh=mesh,
        in_specs=(split, split, split, split, P(tokens)),
        out_specs=(split, split, split, split),
        check_vma=False,
    )
```

```python
import functools
import math

import jax
import jax.numpy as jnp
from jax import lax
from jax.experimental import pallas as pl
from jax.experimental.pallas import tpu as pltpu
from jax.sharding import PartitionSpec as P

HEAD = 128
HEADS = 8
RUN = 64
ROWS = RUN * HEADS
TOK = 128
TAIL = 16
SIDE = 4
UNITS = 2 * SIDE
BLOCKS = 64
CHUNK = 1024
GRAIN = 1024
SCALE = HEAD**-0.5
SCALE2 = SCALE * math.log2(math.e)
NEG = -1e30

bf16 = jnp.bfloat16
f32 = jnp.float32


def dot(a, b):
    return lax.dot_general(a, b, (((1,), (0,)), ((), ())), preferred_element_type=f32)


def dot_t0(a, b):
    return lax.dot_general(a, b, (((0,), (0,)), ((), ())), preferred_element_type=f32)


def attention_kernel(*refs):
    core_ref = refs[0]
    q_refs, do_refs = refs[1:3], refs[3:5]
    kv_refs = refs[5:9]
    out_refs, gq_refs = refs[9:11], refs[11:13]
    dkv_refs = refs[13:17]
    (ids_v, ids_s, kv, qs, dos, outs, gqs, ka, va, qn, qt, don, dot_t, sbuf, wbuf) = refs[17:32]
    (dka, dva, kv_sem, q_sem, ids_sem, out_sem) = refs[32:]
    tokens = BLOCKS * RUN
    step = TOK + TAIL
    width = HEADS * HEAD

    kv_copies = [
        pltpu.make_async_copy(kv_refs[part], kv.at[part], kv_sem.at[part]) for part in range(SIDE)
    ]
    own_columns = pl.ds(pl.multiple_of(core_ref[0] * width, width), width)
    q_copies = [
        pltpu.make_async_copy(q_refs[0].at[:, own_columns], qs.at[0:TOK], q_sem.at[0]),
        pltpu.make_async_copy(q_refs[1], qs.at[TOK : 2 * TOK], q_sem.at[1]),
        pltpu.make_async_copy(do_refs[0].at[:, own_columns], dos.at[0:TOK], q_sem.at[2]),
        pltpu.make_async_copy(do_refs[1], dos.at[TOK : 2 * TOK], q_sem.at[3]),
    ]
    for copy in kv_copies + q_copies:
        copy.start()

    lane = lax.broadcasted_iota(jnp.int32, (RUN, HEAD), 1)
    sub = lax.broadcasted_iota(jnp.int32, (RUN, HEAD), 0)
    diff = jnp.where(lane < RUN, sub - lane, -(1 << 30))
    ones3 = jnp.where(lax.broadcasted_iota(jnp.int32, (CHUNK, HEAD), 1) < 3, 1.0, 0.0).astype(bf16)
    token_of = lax.broadcasted_iota(jnp.int32, (HEAD, ROWS), 1) & (RUN - 1)
    depth_of = lax.broadcasted_iota(jnp.int32, (HEAD, ROWS), 0)
    qt[HEAD : 2 * HEAD, :] = jnp.where(token_of == depth_of, 1.0, 0.0).astype(bf16)

    @pl.loop(0, tokens // CHUNK)
    def _(c):
        s = pl.ds(pl.multiple_of(c * CHUNK, CHUNK), CHUNK)
        va[s, HEAD : 2 * HEAD] = ones3
        dka[s, :] = jnp.zeros((CHUNK, HEAD), f32)
        dva[s, :] = jnp.zeros((CHUNK, HEAD), f32)

    for part in range(SIDE):
        kv_copies[part].wait()
        for unit in range(UNITS):
            tail = kv[part, unit * step + TOK : (unit + 1) * step, 0:HEAD]
            row = part * UNITS + unit
            ids_v[row : row + 1, :] = tail.astype(f32)[0:1, :].astype(jnp.int32)
    fetch = pltpu.make_async_copy(ids_v, ids_s, ids_sem)
    fetch.start()
    fetch.wait()

    for part in range(SIDE):
        for unit in range(UNITS):
            for run in range(2):
                where = ids_s[part * UNITS + unit, run]
                place = pl.ds(pl.multiple_of(where * RUN, RUN), RUN)
                first = unit * step + run * RUN
                ka[place, 0:HEAD] = kv[part, first : first + RUN, 0:HEAD]
                va[place, 0:HEAD] = kv[part, first : first + RUN, HEAD : 2 * HEAD]

    for copy in q_copies:
        copy.wait()

    def run_block(a, position, length):
        rows = pl.ds(pl.multiple_of(a * RUN, RUN), RUN)
        for h in range(HEADS):
            qn[h * RUN : (h + 1) * RUN, :] = qs[rows, h * HEAD : (h + 1) * HEAD]
            don[h * RUN : (h + 1) * RUN, :] = dos[rows, h * HEAD : (h + 1) * HEAD]
        qt[0:HEAD, :] = jnp.transpose(qn[...])
        for j in range(length // RUN):
            mask = jnp.where(diff <= (position - j) * RUN, 0.0, NEG).astype(bf16)
            ka[j * RUN : (j + 1) * RUN, HEAD : 2 * HEAD] = mask
        scores = dot(ka[0:length, :], qt[...]) * SCALE2
        sbuf[0:length, :] = scores
        largest = jnp.max(scores.reshape(length // 8, 8, ROWS), axis=0)
        row_max = jnp.max(largest, axis=0, keepdims=True)
        weights = jnp.exp2(sbuf[0:length, :] - row_max).astype(bf16)
        wbuf[0:length, :] = weights
        mixed = dot_t0(va[0:length, 0:HEAD + TAIL], weights)
        inverse = 1.0 / mixed[HEAD : HEAD + 1, :]
        out_t = (mixed[0:HEAD, :] * inverse).astype(bf16)
        out_n = jnp.transpose(out_t)
        do_t = (jnp.transpose(don[...]).astype(f32) * inverse).astype(bf16)
        don[...] = jnp.transpose(do_t)
        delta = -jnp.sum(do_t.astype(f32) * out_t.astype(f32), axis=0, keepdims=True)
        high = delta.astype(bf16).astype(f32)
        middle = (delta - high).astype(bf16).astype(f32)
        low = delta - high - middle
        dot_t[0:HEAD, :] = do_t
        dot_t[HEAD : 2 * HEAD, :] = jnp.where(
            depth_of == 0,
            high,
            jnp.where(depth_of == 1, middle, jnp.where(depth_of == 2, low, 0.0)),
        ).astype(bf16)
        for h in range(HEADS):
            outs[rows, h * HEAD : (h + 1) * HEAD] = out_n[h * RUN : (h + 1) * RUN, :]
        weights = wbuf[0:length, :]
        dscore = weights * dot(va[0:length, :], dot_t[...]).astype(bf16)
        dva[0:length, :] += dot(weights, don[...])
        dka[0:length, :] += dot(dscore, qn[...])
        grad_n = jnp.transpose((dot_t0(ka[0:length, 0:HEAD], dscore) * SCALE).astype(bf16))
        for h in range(HEADS):
            gqs[rows, h * HEAD : (h + 1) * HEAD] = grad_n[h * RUN : (h + 1) * RUN, :]

    @pl.loop(0, 4)
    def _(a):
        position = ids_s[a // 2, a % 2]
        level = position * RUN // GRAIN
        for n in range(tokens // GRAIN):

            @pl.when(level == n)
            def _():
                run_block(a, position, (n + 1) * GRAIN)

    copies = []
    for half in (1, 0):
        place = slice(half * TOK, (half + 1) * TOK)
        copies.append(pltpu.make_async_copy(outs.at[place], out_refs[half], out_sem.at[half]))
        copies.append(pltpu.make_async_copy(gqs.at[place], gq_refs[half], out_sem.at[2 + half]))
        copies[-2].start()
        copies[-1].start()
    for part in PART_ORDER:
        for unit in range(UNITS):
            for run in range(2):
                where = ids_s[part * UNITS + unit, run]
                place = pl.ds(pl.multiple_of(where * RUN, RUN), RUN)
                first = unit * TOK + run * RUN
                dkv_refs[part][first : first + RUN, 0:HEAD] = (dka[place, :] * SCALE).astype(bf16)
                dkv_refs[part][first : first + RUN, HEAD : 2 * HEAD] = dva[place, :].astype(bf16)
    for copy in copies:
        copy.wait()


PART_ORDER = (1, 2, 3, 0)


def attention(core, q, do, kv):
    anywhere = pl.BlockSpec(memory_space=pl.ANY)
    local = pl.BlockSpec(memory_space=pltpu.VMEM)
    smem = pl.BlockSpec(memory_space=pltpu.SMEM)
    tokens = BLOCKS * RUN
    width = HEADS * HEAD
    wide = jax.ShapeDtypeStruct((TOK, width), bf16)
    part = pltpu.VMEM((UNITS * TOK, 2 * HEAD), bf16)
    near = pltpu.VMEM((TOK, width), bf16)
    return pl.pallas_call(
        attention_kernel,
        out_shape=(wide, near, wide, near) + (part,) * SIDE,
        in_specs=[smem] + [anywhere] * 8,
        out_specs=(anywhere, local, anywhere, local) + (local,) * SIDE,
        scratch_shapes=[
            pltpu.VMEM((32, HEAD), jnp.int32),
            pltpu.SMEM((32, HEAD), jnp.int32),
            pltpu.VMEM((SIDE, UNITS * (TOK + TAIL), 2 * HEAD), bf16),
            pltpu.VMEM((2 * TOK, width), bf16),
            pltpu.VMEM((2 * TOK, width), bf16),
            pltpu.VMEM((2 * TOK, width), bf16),
            pltpu.VMEM((2 * TOK, width), bf16),
            pltpu.VMEM((tokens, 2 * HEAD), bf16),
            pltpu.VMEM((tokens, 2 * HEAD), bf16),
            pltpu.VMEM((ROWS, HEAD), bf16),
            pltpu.VMEM((2 * HEAD, ROWS), bf16),
            pltpu.VMEM((ROWS, HEAD), bf16),
            pltpu.VMEM((2 * HEAD, ROWS), bf16),
            pltpu.VMEM((tokens, ROWS), f32),
            pltpu.VMEM((tokens, ROWS), bf16),
            pltpu.VMEM((tokens, HEAD), f32),
            pltpu.VMEM((tokens, HEAD), f32),
            pltpu.SemaphoreType.DMA((SIDE,)),
            pltpu.SemaphoreType.DMA((4,)),
            pltpu.SemaphoreType.DMA,
            pltpu.SemaphoreType.DMA((4,)),
        ],
        compiler_params=pltpu.CompilerParams(vmem_limit_bytes=VLIMIT * 2**20),
        name="attention",
    )(core, *q, *do, *kv)


VLIMIT = 42


def swap(x):
    return lax.ppermute(x, ("outer", "inner"), [(i, (i + 16) % 32) for i in range(32)])


def shift(x, stage, distance):
    pairs = []
    for core in range(2):
        for z in range(SIDE):
            for y in range(SIDE):
                if core == stage:
                    far = z * SIDE + (y + distance) % SIDE
                else:
                    far = (z + distance) % SIDE * SIDE + y
                pairs.append((core * 16 + z * SIDE + y, core * 16 + far))
    return lax.ppermute(x, ("outer", "inner"), pairs)


def body(queries, keys, values, output_cotangent, positions):
    core = lax.axis_index("outer")

    def pick(x, which):
        width = x.shape[1] // 2
        return lax.dynamic_slice_in_dim(x, which * width, width, axis=1)

    run_ids = jnp.concatenate([positions[0:1], positions[RUN : RUN + 1]]) // RUN
    tail = jnp.zeros((TAIL, 2 * HEAD), bf16).at[0, 0:2].set(run_ids.astype(bf16))

    def unit(which):
        return jnp.concatenate(
            [jnp.concatenate([pick(keys, which), pick(values, which)], 1), tail], 0
        )

    kv_own = jnp.concatenate([unit(core), swap(unit(1 - core))], 0)
    line = [kv_own] + [shift(kv_own, 0, d) for d in ORDER]
    line = lax.optimization_barrier(tuple(line) + (queries, output_cotangent))
    queries, output_cotangent = line[4:]
    line = jnp.concatenate(line[:4], 0)
    lines = [line] + [shift(line, 1, d) for d in ORDER]
    q_other = swap(pick(queries, 1 - core))
    do_other = swap(pick(output_cotangent, 1 - core))

    results = attention(
        core.astype(jnp.int32).reshape(1),
        (queries, q_other),
        (output_cotangent, do_other),
        lines,
    )
    outs, grads, parts = results[:2], results[2:4], results[4:]

    def total(terms):
        return functools.reduce(jnp.add, [t.astype(f32) for t in terms]).astype(bf16)

    def cut(x, i):
        return x[i * 2 * TOK : (i + 1) * 2 * TOK]

    line = total([parts[0]] + [shift(parts[1 + i], 1, -d) for i, d in enumerate(ORDER)])
    dkv = total([cut(line, 0)] + [shift(cut(line, 1 + i), 0, -d) for i, d in enumerate(ORDER)])
    dkv_mine, dkv_other = dkv[:TOK], swap(dkv[TOK:])

    def join(mine, other):
        return jnp.where(
            core == 0, jnp.concatenate([mine, other], 1), jnp.concatenate([other, mine], 1)
        )

    attn_out = join(outs[0], swap(outs[1]))
    grad_queries = join(grads[0], swap(grads[1]))
    key_gradient = join(dkv_mine[:, :HEAD], dkv_other[:, :HEAD])
    value_gradient = join(dkv_mine[:, HEAD:], dkv_other[:, HEAD:])
    return attn_out, grad_queries, key_gradient, value_gradient


ORDER = (2, 1, 3)


def solution(mesh):
    tokens = ("outer", "inner")
    split = P(tokens, "head")
    return jax.shard_map(
        body,
        mesh=mesh,
        in_specs=(split, split, split, split, P(tokens)),
        out_specs=(split, split, split, split),
        check_vma=False,
    )
```

```python
import functools
import math

import jax
import jax.numpy as jnp
from jax import lax
from jax.experimental import pallas as pl
from jax.experimental.pallas import tpu as pltpu
from jax.sharding import PartitionSpec as P

HEAD = 128
HEADS = 8
RUN = 64
ROWS = RUN * HEADS
TOK = 128
TAIL = 16
SIDE = 4
UNITS = 2 * SIDE
BLOCKS = 64
CHUNK = 1024
LENGTHS = (1024, 2048, 2560, 3072, 3584, 4096)
SCALE = HEAD**-0.5
SCALE2 = SCALE * math.log2(math.e)
NEG = -1e30

bf16 = jnp.bfloat16
f32 = jnp.float32


def dot(a, b):
    return lax.dot_general(a, b, (((1,), (0,)), ((), ())), preferred_element_type=f32)


def dot_t0(a, b):
    return lax.dot_general(a, b, (((0,), (0,)), ((), ())), preferred_element_type=f32)


def attention_kernel(*refs):
    core_ref = refs[0]
    q_refs, do_refs = refs[1:3], refs[3:5]
    kv_refs = refs[5:9]
    out_refs, gq_refs = refs[9:11], refs[11:13]
    dkv_refs = refs[13:17]
    (ids_v, ids_s, kv, qs, dos, outs, gqs, dkv, ka, va, qn, qt, don, dot_t, sbuf, wbuf) = refs[17:33]
    (dka, dva, kv_sem, q_sem, ids_sem, out_sem, dkv_sem) = refs[33:]
    tokens = BLOCKS * RUN
    step = TOK + TAIL
    width = HEADS * HEAD

    kv_copies = [
        pltpu.make_async_copy(kv_refs[part], kv.at[part], kv_sem.at[part]) for part in range(SIDE)
    ]
    own_columns = pl.ds(pl.multiple_of(core_ref[0] * width, width), width)
    q_copies = [
        pltpu.make_async_copy(q_refs[0].at[:, own_columns], qs.at[0:TOK], q_sem.at[0]),
        pltpu.make_async_copy(q_refs[1], qs.at[TOK : 2 * TOK], q_sem.at[1]),
        pltpu.make_async_copy(do_refs[0].at[:, own_columns], dos.at[0:TOK], q_sem.at[2]),
        pltpu.make_async_copy(do_refs[1], dos.at[TOK : 2 * TOK], q_sem.at[3]),
    ]
    for copy in kv_copies + q_copies:
        copy.start()

    lane = lax.broadcasted_iota(jnp.int32, (RUN, HEAD), 1)
    sub = lax.broadcasted_iota(jnp.int32, (RUN, HEAD), 0)
    diff = jnp.where(lane < RUN, sub - lane, -(1 << 30))
    ones3 = jnp.where(lax.broadcasted_iota(jnp.int32, (CHUNK, HEAD), 1) < 3, 1.0, 0.0).astype(bf16)
    token_of = lax.broadcasted_iota(jnp.int32, (HEAD, ROWS), 1) & (RUN - 1)
    depth_of = lax.broadcasted_iota(jnp.int32, (HEAD, ROWS), 0)
    qt[HEAD : 2 * HEAD, :] = jnp.where(token_of == depth_of, 1.0, 0.0).astype(bf16)

    @pl.loop(0, tokens // CHUNK)
    def _(c):
        s = pl.ds(pl.multiple_of(c * CHUNK, CHUNK), CHUNK)
        va[s, HEAD : 2 * HEAD] = ones3
        dka[s, :] = jnp.zeros((CHUNK, HEAD), f32)
        dva[s, :] = jnp.zeros((CHUNK, HEAD), f32)

    for part in range(SIDE):
        kv_copies[part].wait()
        for unit in range(UNITS):
            tail = kv[part, unit * step + TOK : (unit + 1) * step, 0:HEAD]
            row = part * UNITS + unit
            ids_v[row : row + 1, :] = tail.astype(f32)[0:1, :].astype(jnp.int32)
    fetch = pltpu.make_async_copy(ids_v, ids_s, ids_sem)
    fetch.start()
    fetch.wait()

    for part in range(SIDE):
        for unit in range(UNITS):
            for run in range(2):
                where = ids_s[part * UNITS + unit, run]
                place = pl.ds(pl.multiple_of(where * RUN, RUN), RUN)
                first = unit * step + run * RUN
                ka[place, 0:HEAD] = kv[part, first : first + RUN, 0:HEAD]
                va[place, 0:HEAD] = kv[part, first : first + RUN, HEAD : 2 * HEAD]

    for copy in q_copies:
        copy.wait()

    def run_block(a, position, length):
        rows = pl.ds(pl.multiple_of(a * RUN, RUN), RUN)
        for h in range(HEADS):
            qn[h * RUN : (h + 1) * RUN, :] = qs[rows, h * HEAD : (h + 1) * HEAD]
            don[h * RUN : (h + 1) * RUN, :] = dos[rows, h * HEAD : (h + 1) * HEAD]
        qt[0:HEAD, :] = jnp.transpose(qn[...])
        for j in range(length // RUN):
            mask = jnp.where(diff <= (position - j) * RUN, 0.0, NEG).astype(bf16)
            ka[j * RUN : (j + 1) * RUN, HEAD : 2 * HEAD] = mask
        scores = dot(ka[0:length, :], qt[...]) * SCALE2
        sbuf[0:length, :] = scores
        largest = jnp.max(scores.reshape(length // 8, 8, ROWS), axis=0)
        row_max = jnp.max(largest, axis=0, keepdims=True)
        weights = jnp.exp2(sbuf[0:length, :] - row_max).astype(bf16)
        wbuf[0:length, :] = weights
        mixed = dot_t0(va[0:length, 0:HEAD + TAIL], weights)
        inverse = 1.0 / mixed[HEAD : HEAD + 1, :]
        out_t = (mixed[0:HEAD, :] * inverse).astype(bf16)
        out_n = jnp.transpose(out_t)
        do_t = (jnp.transpose(don[...]).astype(f32) * inverse).astype(bf16)
        don[...] = jnp.transpose(do_t)
        delta = -jnp.sum(do_t.astype(f32) * out_t.astype(f32), axis=0, keepdims=True)
        high = delta.astype(bf16).astype(f32)
        middle = (delta - high).astype(bf16).astype(f32)
        low = delta - high - middle
        dot_t[0:HEAD, :] = do_t
        dot_t[HEAD : 2 * HEAD, :] = jnp.where(
            depth_of == 0,
            high,
            jnp.where(depth_of == 1, middle, jnp.where(depth_of == 2, low, 0.0)),
        ).astype(bf16)
        for h in range(HEADS):
            outs[rows, h * HEAD : (h + 1) * HEAD] = out_n[h * RUN : (h + 1) * RUN, :]
        weights = wbuf[0:length, :]
        dscore = weights * dot(va[0:length, :], dot_t[...]).astype(bf16)
        dva[0:length, :] += dot(weights, don[...])
        dka[0:length, :] += dot(dscore, qn[...])
        grad_n = jnp.transpose((dot_t0(ka[0:length, 0:HEAD], dscore) * SCALE).astype(bf16))
        for h in range(HEADS):
            gqs[rows, h * HEAD : (h + 1) * HEAD] = grad_n[h * RUN : (h + 1) * RUN, :]

    @pl.loop(0, 4)
    def _(a):
        position = ids_s[a // 2, a % 2]
        needed = (position + 1) * RUN
        for short, length in zip((0,) + LENGTHS, LENGTHS):

            @pl.when((needed > short) & (needed <= length))
            def _():
                run_block(a, position, length)

    copies = []
    for half in range(2):
        place = slice(half * TOK, (half + 1) * TOK)
        copies.append(pltpu.make_async_copy(outs.at[place], out_refs[half], out_sem.at[half]))
        copies.append(pltpu.make_async_copy(gqs.at[place], gq_refs[half], out_sem.at[2 + half]))
        copies[-2].start()
        copies[-1].start()
    for part in PART_ORDER:
        for unit in range(UNITS):
            for run in range(2):
                where = ids_s[part * UNITS + unit, run]
                place = pl.ds(pl.multiple_of(where * RUN, RUN), RUN)
                first = unit * TOK + run * RUN
                dkv[part, first : first + RUN, 0:HEAD] = (dka[place, :] * SCALE).astype(bf16)
                dkv[part, first : first + RUN, HEAD : 2 * HEAD] = dva[place, :].astype(bf16)
        copies.append(pltpu.make_async_copy(dkv.at[part], dkv_refs[part], dkv_sem.at[part]))
        copies[-1].start()
    for copy in copies:
        copy.wait()


PART_ORDER = (1, 2, 3, 0)


def attention(core, q, do, kv):
    anywhere = pl.BlockSpec(memory_space=pl.ANY)
    smem = pl.BlockSpec(memory_space=pltpu.SMEM)
    tokens = BLOCKS * RUN
    width = HEADS * HEAD
    wide = pltpu.HBM((TOK, width), bf16)
    part = pltpu.HBM((UNITS * TOK, 2 * HEAD), bf16)
    return pl.pallas_call(
        attention_kernel,
        out_shape=(wide,) * 4 + (part,) * SIDE,
        in_specs=[smem] + [anywhere] * 8,
        out_specs=(pl.BlockSpec(memory_space=pltpu.HBM),) * 8,
        scratch_shapes=[
            pltpu.VMEM((32, HEAD), jnp.int32),
            pltpu.SMEM((32, HEAD), jnp.int32),
            pltpu.VMEM((SIDE, UNITS * (TOK + TAIL), 2 * HEAD), bf16),
            pltpu.VMEM((2 * TOK, width), bf16),
            pltpu.VMEM((2 * TOK, width), bf16),
            pltpu.VMEM((2 * TOK, width), bf16),
            pltpu.VMEM((2 * TOK, width), bf16),
            pltpu.VMEM((SIDE, UNITS * TOK, 2 * HEAD), bf16),
            pltpu.VMEM((tokens, 2 * HEAD), bf16),
            pltpu.VMEM((tokens, 2 * HEAD), bf16),
            pltpu.VMEM((ROWS, HEAD), bf16),
            pltpu.VMEM((2 * HEAD, ROWS), bf16),
            pltpu.VMEM((ROWS, HEAD), bf16),
            pltpu.VMEM((2 * HEAD, ROWS), bf16),
            pltpu.VMEM((tokens, ROWS), f32),
            pltpu.VMEM((tokens, ROWS), bf16),
            pltpu.VMEM((tokens, HEAD), f32),
            pltpu.VMEM((tokens, HEAD), f32),
            pltpu.SemaphoreType.DMA((SIDE,)),
            pltpu.SemaphoreType.DMA((4,)),
            pltpu.SemaphoreType.DMA,
            pltpu.SemaphoreType.DMA((4,)),
            pltpu.SemaphoreType.DMA((SIDE,)),
        ],
        compiler_params=pltpu.CompilerParams(vmem_limit_bytes=VLIMIT * 2**20),
        name="attention",
    )(core, *q, *do, *kv)


VLIMIT = 42


def unit_kernel(core_ref, where_hbm, keys_hbm, values_hbm, mine_ref, other_ref, where, keys, values, sem):
    copies = [
        pltpu.make_async_copy(where_hbm, where, sem.at[0]),
        pltpu.make_async_copy(keys_hbm, keys, sem.at[1]),
        pltpu.make_async_copy(values_hbm, values, sem.at[2]),
    ]
    for copy in copies:
        copy.start()
    for copy in copies:
        copy.wait()
    lane = lax.broadcasted_iota(jnp.int32, (TAIL, 2 * HEAD), 1)
    first, second = where[0] // RUN, where[RUN] // RUN
    tail = jnp.where(lane == 0, first, jnp.where(lane == 1, second, 0)).astype(f32).astype(bf16)
    mine_ref[TOK : TOK + TAIL, :] = tail
    other_ref[TOK : TOK + TAIL, :] = tail

    def fill(low_ref, high_ref):
        low_ref[0:TOK, 0:HEAD] = keys[:, 0:HEAD]
        low_ref[0:TOK, HEAD : 2 * HEAD] = values[:, 0:HEAD]
        high_ref[0:TOK, 0:HEAD] = keys[:, HEAD : 2 * HEAD]
        high_ref[0:TOK, HEAD : 2 * HEAD] = values[:, HEAD : 2 * HEAD]

    @pl.when(core_ref[0] == 0)
    def _():
        fill(mine_ref, other_ref)

    @pl.when(core_ref[0] != 0)
    def _():
        fill(other_ref, mine_ref)


def key_units(core, positions, keys, values):
    vmem = pl.BlockSpec(memory_space=pltpu.VMEM)
    hbm = pl.BlockSpec(memory_space=pltpu.HBM)
    unit = jax.ShapeDtypeStruct((TOK + TAIL, 2 * HEAD), bf16)
    return pl.pallas_call(
        unit_kernel,
        out_shape=(unit, unit),
        in_specs=[pl.BlockSpec(memory_space=pltpu.SMEM), hbm, hbm, hbm],
        out_specs=(vmem, vmem),
        scratch_shapes=[
            pltpu.SMEM((TOK,), jnp.int32),
            pltpu.VMEM((TOK, 2 * HEAD), bf16),
            pltpu.VMEM((TOK, 2 * HEAD), bf16),
            pltpu.SemaphoreType.DMA((3,)),
        ],
        compiler_params=pltpu.CompilerParams(vmem_limit_bytes=8 * 2**20),
        name="units",
    )(core, positions, keys, values)


def swap(x):
    return lax.ppermute(x, ("outer", "inner"), [(i, (i + 16) % 32) for i in range(32)])


def shift(x, stage, distance):
    pairs = []
    for core in range(2):
        for z in range(SIDE):
            for y in range(SIDE):
                if core == stage:
                    far = z * SIDE + (y + distance) % SIDE
                else:
                    far = (z + distance) % SIDE * SIDE + y
                pairs.append((core * 16 + z * SIDE + y, core * 16 + far))
    return lax.ppermute(x, ("outer", "inner"), pairs)


def body(queries, keys, values, output_cotangent, positions):
    core = lax.axis_index("outer")

    def pick(x, which):
        width = x.shape[1] // 2
        return lax.dynamic_slice_in_dim(x, which * width, width, axis=1)

    core_index = core.astype(jnp.int32).reshape(1)
    kv_mine, kv_other = key_units(core_index, positions, keys, values)
    kv_own = jnp.concatenate([kv_mine, swap(kv_other)], 0)
    line = [kv_own] + [shift(kv_own, 0, d) for d in ORDER]
    line = lax.optimization_barrier(tuple(line) + (queries, output_cotangent))
    queries, output_cotangent = line[4:]
    line = jnp.concatenate(line[:4], 0)
    lines = [line] + [shift(line, 1, d) for d in ORDER]
    q_other = swap(pick(queries, 1 - core))
    do_other = swap(pick(output_cotangent, 1 - core))

    results = attention(
        core_index,
        (queries, q_other),
        (output_cotangent, do_other),
        lines,
    )
    outs, grads, parts = results[:2], results[2:4], results[4:]

    def total(terms):
        return functools.reduce(jnp.add, [t.astype(f32) for t in terms]).astype(bf16)

    def cut(x, i):
        return x[i * 2 * TOK : (i + 1) * 2 * TOK]

    line = total([parts[0]] + [shift(parts[1 + i], 1, -d) for i, d in enumerate(ORDER)])
    dkv = total([cut(line, 0)] + [shift(cut(line, 1 + i), 0, -d) for i, d in enumerate(ORDER)])
    dkv_mine, dkv_other = dkv[:TOK], swap(dkv[TOK:])

    def join(mine, other):
        return jnp.where(
            core == 0, jnp.concatenate([mine, other], 1), jnp.concatenate([other, mine], 1)
        )

    attn_out = join(outs[0], swap(outs[1]))
    grad_queries = join(grads[0], swap(grads[1]))
    key_gradient = join(dkv_mine[:, :HEAD], dkv_other[:, :HEAD])
    value_gradient = join(dkv_mine[:, HEAD:], dkv_other[:, HEAD:])
    return attn_out, grad_queries, key_gradient, value_gradient


ORDER = (2, 1, 3)


def solution(mesh):
    tokens = ("outer", "inner")
    split = P(tokens, "head")
    return jax.shard_map(
        body,
        mesh=mesh,
        in_specs=(split, split, split, split, P(tokens)),
        out_specs=(split, split, split, split),
        check_vma=False,
    )
```

```python
import functools
import math

import jax
import jax.numpy as jnp
from jax import lax
from jax.experimental import pallas as pl
from jax.experimental.pallas import tpu as pltpu
from jax.sharding import PartitionSpec as P

HEAD = 128
HEADS = 8
RUN = 64
ROWS = RUN * HEADS
TOK = 128
TAIL = 16
SIDE = 4
UNITS = 2 * SIDE
BLOCKS = 64
CHUNK = 1024
LENGTHS = (1024, 2048, 2560, 3072, 3584, 4096)
SCALE = HEAD**-0.5
SCALE2 = SCALE * math.log2(math.e)
NEG = -1e30

bf16 = jnp.bfloat16
f32 = jnp.float32


def dot(a, b):
    return lax.dot_general(a, b, (((1,), (0,)), ((), ())), preferred_element_type=f32)


def dot_t0(a, b):
    return lax.dot_general(a, b, (((0,), (0,)), ((), ())), preferred_element_type=f32)


def attention_kernel(*refs):
    core_ref = refs[0]
    q_refs, do_refs = refs[1:3], refs[3:5]
    kv_refs = refs[5:9]
    out_refs, gq_refs = refs[9:11], refs[11:13]
    dkv_refs = refs[13:17]
    (ids_v, ids_s, outs, gqs, dkv, ka, va, qn, qt, don, dot_t, sbuf, wbuf) = refs[17:30]
    (dka, dva, ids_sem, out_sem, dkv_sem) = refs[30:]
    tokens = BLOCKS * RUN
    step = TOK + TAIL
    width = HEADS * HEAD

    lane = lax.broadcasted_iota(jnp.int32, (RUN, HEAD), 1)
    sub = lax.broadcasted_iota(jnp.int32, (RUN, HEAD), 0)
    diff = jnp.where(lane < RUN, sub - lane, -(1 << 30))
    ones3 = jnp.where(lax.broadcasted_iota(jnp.int32, (CHUNK, HEAD), 1) < 3, 1.0, 0.0).astype(bf16)
    token_of = lax.broadcasted_iota(jnp.int32, (HEAD, ROWS), 1) & (RUN - 1)
    depth_of = lax.broadcasted_iota(jnp.int32, (HEAD, ROWS), 0)
    qt[HEAD : 2 * HEAD, :] = jnp.where(token_of == depth_of, 1.0, 0.0).astype(bf16)

    @pl.loop(0, tokens // CHUNK)
    def _(c):
        s = pl.ds(pl.multiple_of(c * CHUNK, CHUNK), CHUNK)
        va[s, HEAD : 2 * HEAD] = ones3
        dka[s, :] = jnp.zeros((CHUNK, HEAD), f32)
        dva[s, :] = jnp.zeros((CHUNK, HEAD), f32)

    for part in range(SIDE):
        for unit in range(UNITS):
            tail = kv_refs[part][unit * step + TOK : (unit + 1) * step, 0:HEAD]
            row = part * UNITS + unit
            ids_v[row : row + 1, :] = tail.astype(f32)[0:1, :].astype(jnp.int32)
    fetch = pltpu.make_async_copy(ids_v, ids_s, ids_sem)
    fetch.start()
    fetch.wait()

    for part in range(SIDE):
        for unit in range(UNITS):
            for run in range(2):
                where = ids_s[part * UNITS + unit, run]
                place = pl.ds(pl.multiple_of(where * RUN, RUN), RUN)
                first = unit * step + run * RUN
                ka[place, 0:HEAD] = kv_refs[part][first : first + RUN, 0:HEAD]
                va[place, 0:HEAD] = kv_refs[part][first : first + RUN, HEAD : 2 * HEAD]

    def run_block(a, position, length):
        rows = pl.ds(pl.multiple_of(a * RUN, RUN), RUN)
        qt[0:HEAD, :] = jnp.transpose(qn[...])
        for j in range(length // RUN):
            mask = jnp.where(diff <= (position - j) * RUN, 0.0, NEG).astype(bf16)
            ka[j * RUN : (j + 1) * RUN, HEAD : 2 * HEAD] = mask
        scores = dot(ka[0:length, :], qt[...]) * SCALE2
        sbuf[0:length, :] = scores
        largest = jnp.max(scores.reshape(length // 8, 8, ROWS), axis=0)
        row_max = jnp.max(largest, axis=0, keepdims=True)
        weights = jnp.exp2(sbuf[0:length, :] - row_max).astype(bf16)
        wbuf[0:length, :] = weights
        mixed = dot_t0(va[0:length, 0:HEAD + TAIL], weights)
        inverse = 1.0 / mixed[HEAD : HEAD + 1, :]
        out_t = (mixed[0:HEAD, :] * inverse).astype(bf16)
        out_n = jnp.transpose(out_t)
        do_t = (jnp.transpose(don[...]).astype(f32) * inverse).astype(bf16)
        don[...] = jnp.transpose(do_t)
        delta = -jnp.sum(do_t.astype(f32) * out_t.astype(f32), axis=0, keepdims=True)
        high = delta.astype(bf16).astype(f32)
        middle = (delta - high).astype(bf16).astype(f32)
        low = delta - high - middle
        dot_t[0:HEAD, :] = do_t
        dot_t[HEAD : 2 * HEAD, :] = jnp.where(
            depth_of == 0,
            high,
            jnp.where(depth_of == 1, middle, jnp.where(depth_of == 2, low, 0.0)),
        ).astype(bf16)
        for h in range(HEADS):
            outs[rows, h * HEAD : (h + 1) * HEAD] = out_n[h * RUN : (h + 1) * RUN, :]
        weights = wbuf[0:length, :]
        dscore = weights * dot(va[0:length, :], dot_t[...]).astype(bf16)
        dva[0:length, :] += dot(weights, don[...])
        dka[0:length, :] += dot(dscore, qn[...])
        grad_n = jnp.transpose((dot_t0(ka[0:length, 0:HEAD], dscore) * SCALE).astype(bf16))
        for h in range(HEADS):
            gqs[rows, h * HEAD : (h + 1) * HEAD] = grad_n[h * RUN : (h + 1) * RUN, :]

    @pl.loop(0, 4)
    def _(a):
        position = ids_s[a // 2, a % 2]
        needed = (position + 1) * RUN
        line = pl.ds(pl.multiple_of(a % 2 * RUN, RUN), RUN)

        def take(q_ref, do_ref, base):
            for h in range(HEADS):
                columns = pl.ds(pl.multiple_of(base + h * HEAD, HEAD), HEAD)
                qn[h * RUN : (h + 1) * RUN, :] = q_ref[line, columns]
                don[h * RUN : (h + 1) * RUN, :] = do_ref[line, columns]

        @pl.when(a < 2)
        def _():
            take(q_refs[0], do_refs[0], core_ref[0] * width)

        @pl.when(a >= 2)
        def _():
            take(q_refs[1], do_refs[1], 0)

        for short, length in zip((0,) + LENGTHS, LENGTHS):

            @pl.when((needed > short) & (needed <= length))
            def _():
                run_block(a, position, length)

    copies = []
    for half in range(2):
        place = slice(half * TOK, (half + 1) * TOK)
        copies.append(pltpu.make_async_copy(outs.at[place], out_refs[half], out_sem.at[half]))
        copies.append(pltpu.make_async_copy(gqs.at[place], gq_refs[half], out_sem.at[2 + half]))
        copies[-2].start()
        copies[-1].start()
    for part in PART_ORDER:
        for unit in range(UNITS):
            for run in range(2):
                where = ids_s[part * UNITS + unit, run]
                place = pl.ds(pl.multiple_of(where * RUN, RUN), RUN)
                first = unit * TOK + run * RUN
                dkv[part, first : first + RUN, 0:HEAD] = (dka[place, :] * SCALE).astype(bf16)
                dkv[part, first : first + RUN, HEAD : 2 * HEAD] = dva[place, :].astype(bf16)
        copies.append(pltpu.make_async_copy(dkv.at[part], dkv_refs[part], dkv_sem.at[part]))
        copies[-1].start()
    for copy in copies:
        copy.wait()


PART_ORDER = (1, 2, 3, 0)


def attention(core, q, do, kv):
    local = pl.BlockSpec(memory_space=pltpu.VMEM)
    smem = pl.BlockSpec(memory_space=pltpu.SMEM)
    tokens = BLOCKS * RUN
    width = HEADS * HEAD
    wide = pltpu.HBM((TOK, width), bf16)
    part = pltpu.HBM((UNITS * TOK, 2 * HEAD), bf16)
    return pl.pallas_call(
        attention_kernel,
        out_shape=(wide,) * 4 + (part,) * SIDE,
        in_specs=[smem] + [local] * 8,
        out_specs=(pl.BlockSpec(memory_space=pltpu.HBM),) * 8,
        scratch_shapes=[
            pltpu.VMEM((32, HEAD), jnp.int32),
            pltpu.SMEM((32, HEAD), jnp.int32),
            pltpu.VMEM((2 * TOK, width), bf16),
            pltpu.VMEM((2 * TOK, width), bf16),
            pltpu.VMEM((SIDE, UNITS * TOK, 2 * HEAD), bf16),
            pltpu.VMEM((tokens, 2 * HEAD), bf16),
            pltpu.VMEM((tokens, 2 * HEAD), bf16),
            pltpu.VMEM((ROWS, HEAD), bf16),
            pltpu.VMEM((2 * HEAD, ROWS), bf16),
            pltpu.VMEM((ROWS, HEAD), bf16),
            pltpu.VMEM((2 * HEAD, ROWS), bf16),
            pltpu.VMEM((tokens, ROWS), f32),
            pltpu.VMEM((tokens, ROWS), bf16),
            pltpu.VMEM((tokens, HEAD), f32),
            pltpu.VMEM((tokens, HEAD), f32),
            pltpu.SemaphoreType.DMA,
            pltpu.SemaphoreType.DMA((4,)),
            pltpu.SemaphoreType.DMA((SIDE,)),
        ],
        compiler_params=pltpu.CompilerParams(vmem_limit_bytes=VLIMIT * 2**20),
        name="attention",
    )(core, *q, *do, *kv)


VLIMIT = 40


def unit_kernel(core_ref, where_hbm, keys_hbm, values_hbm, mine_ref, other_ref, where, keys, values, sem):
    copies = [
        pltpu.make_async_copy(where_hbm, where, sem.at[0]),
        pltpu.make_async_copy(keys_hbm, keys, sem.at[1]),
        pltpu.make_async_copy(values_hbm, values, sem.at[2]),
    ]
    for copy in copies:
        copy.start()
    for copy in copies:
        copy.wait()
    lane = lax.broadcasted_iota(jnp.int32, (TAIL, 2 * HEAD), 1)
    first, second = where[0] // RUN, where[RUN] // RUN
    tail = jnp.where(lane == 0, first, jnp.where(lane == 1, second, 0)).astype(f32).astype(bf16)
    mine_ref[TOK : TOK + TAIL, :] = tail
    other_ref[TOK : TOK + TAIL, :] = tail

    def fill(low_ref, high_ref):
        low_ref[0:TOK, 0:HEAD] = keys[:, 0:HEAD]
        low_ref[0:TOK, HEAD : 2 * HEAD] = values[:, 0:HEAD]
        high_ref[0:TOK, 0:HEAD] = keys[:, HEAD : 2 * HEAD]
        high_ref[0:TOK, HEAD : 2 * HEAD] = values[:, HEAD : 2 * HEAD]

    @pl.when(core_ref[0] == 0)
    def _():
        fill(mine_ref, other_ref)

    @pl.when(core_ref[0] != 0)
    def _():
        fill(other_ref, mine_ref)


def key_units(core, positions, keys, values):
    vmem = pl.BlockSpec(memory_space=pltpu.VMEM)
    hbm = pl.BlockSpec(memory_space=pltpu.HBM)
    unit = jax.ShapeDtypeStruct((TOK + TAIL, 2 * HEAD), bf16)
    return pl.pallas_call(
        unit_kernel,
        out_shape=(unit, unit),
        in_specs=[pl.BlockSpec(memory_space=pltpu.SMEM), hbm, hbm, hbm],
        out_specs=(vmem, vmem),
        scratch_shapes=[
            pltpu.SMEM((TOK,), jnp.int32),
            pltpu.VMEM((TOK, 2 * HEAD), bf16),
            pltpu.VMEM((TOK, 2 * HEAD), bf16),
            pltpu.SemaphoreType.DMA((3,)),
        ],
        compiler_params=pltpu.CompilerParams(vmem_limit_bytes=8 * 2**20),
        name="units",
    )(core, *(pltpu.with_memory_space_constraint(x, pltpu.HBM) for x in (positions, keys, values)))


def swap(x):
    return lax.ppermute(x, ("outer", "inner"), [(i, (i + 16) % 32) for i in range(32)])


def shift(x, stage, distance):
    pairs = []
    for core in range(2):
        for z in range(SIDE):
            for y in range(SIDE):
                if core == stage:
                    far = z * SIDE + (y + distance) % SIDE
                else:
                    far = (z + distance) % SIDE * SIDE + y
                pairs.append((core * 16 + z * SIDE + y, core * 16 + far))
    return lax.ppermute(x, ("outer", "inner"), pairs)


def body(queries, keys, values, output_cotangent, positions):
    core = lax.axis_index("outer")

    def pick(x, which):
        width = x.shape[1] // 2
        return lax.dynamic_slice_in_dim(x, which * width, width, axis=1)

    core_index = core.astype(jnp.int32).reshape(1)
    kv_mine, kv_other = key_units(core_index, positions, keys, values)
    kv_own = jnp.concatenate([kv_mine, swap(kv_other)], 0)
    line = [kv_own] + [shift(kv_own, 0, d) for d in ORDER]
    line = lax.optimization_barrier(tuple(line) + (queries, output_cotangent))
    queries, output_cotangent = line[4:]
    line = jnp.concatenate(line[:4], 0)
    lines = [line] + [shift(line, 1, d) for d in ORDER]
    q_other = swap(pick(queries, 1 - core))
    do_other = swap(pick(output_cotangent, 1 - core))

    results = attention(
        core_index,
        (queries, q_other),
        (output_cotangent, do_other),
        lines,
    )
    outs, grads, parts = results[:2], results[2:4], results[4:]

    def total(terms):
        return functools.reduce(jnp.add, [t.astype(f32) for t in terms]).astype(bf16)

    def cut(x, i):
        return x[i * 2 * TOK : (i + 1) * 2 * TOK]

    line = total([parts[0]] + [shift(parts[1 + i], 1, -d) for i, d in enumerate(ORDER)])
    dkv = total([cut(line, 0)] + [shift(cut(line, 1 + i), 0, -d) for i, d in enumerate(ORDER)])
    dkv_mine, dkv_other = dkv[:TOK], swap(dkv[TOK:])

    def join(mine, other):
        return jnp.where(
            core == 0, jnp.concatenate([mine, other], 1), jnp.concatenate([other, mine], 1)
        )

    attn_out = join(outs[0], swap(outs[1]))
    grad_queries = join(grads[0], swap(grads[1]))
    key_gradient = join(dkv_mine[:, :HEAD], dkv_other[:, :HEAD])
    value_gradient = join(dkv_mine[:, HEAD:], dkv_other[:, HEAD:])
    return attn_out, grad_queries, key_gradient, value_gradient


ORDER = (2, 1, 3)


def solution(mesh):
    tokens = ("outer", "inner")
    split = P(tokens, "head")
    return jax.shard_map(
        body,
        mesh=mesh,
        in_specs=(split, split, split, split, P(tokens)),
        out_specs=(split, split, split, split),
        check_vma=False,
    )
```

```python
import functools
import math

import jax
import jax.numpy as jnp
from jax import lax
from jax.experimental import pallas as pl
from jax.experimental.pallas import tpu as pltpu
from jax.sharding import PartitionSpec as P

HEAD = 128
HEADS = 8
RUN = 64
ROWS = RUN * HEADS
TOK = 128
TAIL = 16
SIDE = 4
UNITS = 2 * SIDE
BLOCKS = 64
CHUNK = 1024
LENGTHS = (1024, 2048, 2560, 3072, 3584, 4096)
SCALE = HEAD**-0.5
SCALE2 = SCALE * math.log2(math.e)
NEG = -1e30

bf16 = jnp.bfloat16
f32 = jnp.float32


def dot(a, b):
    return lax.dot_general(a, b, (((1,), (0,)), ((), ())), preferred_element_type=f32)


def dot_t0(a, b):
    return lax.dot_general(a, b, (((0,), (0,)), ((), ())), preferred_element_type=f32)


def attention_kernel(*refs):
    core_ref = refs[0]
    q_refs, do_refs = refs[1:3], refs[3:5]
    kv_refs = refs[5:9]
    out_refs, gq_refs = refs[9:11], refs[11:13]
    dkv_refs = refs[13:17]
    (ids_v, ids_s, outs, gqs, dkv, ka, va, qn, qt, don, dot_t, sbuf, wbuf) = refs[17:30]
    (dka, dva, ids_sem, out_sem, dkv_sem) = refs[30:]
    tokens = BLOCKS * RUN
    step = 2 * TOK + TAIL
    width = HEADS * HEAD

    for part in range(SIDE):
        for pair in range(SIDE):
            tail = kv_refs[part][pair * step + 2 * TOK : (pair + 1) * step, 0:HEAD]
            row = part * SIDE + pair
            ids_v[row : row + 1, :] = tail.astype(f32)[0:1, :].astype(jnp.int32)
    fetch = pltpu.make_async_copy(ids_v, ids_s, ids_sem)
    fetch.start()

    lane = lax.broadcasted_iota(jnp.int32, (RUN, HEAD), 1)
    sub = lax.broadcasted_iota(jnp.int32, (RUN, HEAD), 0)
    diff = jnp.where(lane < RUN, sub - lane, -(1 << 30))
    ones3 = jnp.where(lax.broadcasted_iota(jnp.int32, (CHUNK, HEAD), 1) < 3, 1.0, 0.0).astype(bf16)
    token_of = lax.broadcasted_iota(jnp.int32, (HEAD, ROWS), 1) & (RUN - 1)
    depth_of = lax.broadcasted_iota(jnp.int32, (HEAD, ROWS), 0)
    qt[HEAD : 2 * HEAD, :] = jnp.where(token_of == depth_of, 1.0, 0.0).astype(bf16)

    @pl.loop(0, tokens // CHUNK)
    def _(c):
        s = pl.ds(pl.multiple_of(c * CHUNK, CHUNK), CHUNK)
        va[s, HEAD : 2 * HEAD] = ones3
        dka[s, :] = jnp.zeros((CHUNK, HEAD), f32)
        dva[s, :] = jnp.zeros((CHUNK, HEAD), f32)

    fetch.wait()

    for part in range(SIDE):
        for unit in range(UNITS):
            for run in range(2):
                where = ids_s[part * SIDE + unit // 2, unit % 2 * 2 + run]
                place = pl.ds(pl.multiple_of(where * RUN, RUN), RUN)
                first = unit // 2 * step + unit % 2 * TOK + run * RUN
                ka[place, 0:HEAD] = kv_refs[part][first : first + RUN, 0:HEAD]
                va[place, 0:HEAD] = kv_refs[part][first : first + RUN, HEAD : 2 * HEAD]

    def run_block(a, position, length):
        rows = pl.ds(pl.multiple_of(a * RUN, RUN), RUN)
        qt[0:HEAD, :] = jnp.transpose(qn[...])
        for j in range(length // RUN):
            mask = jnp.where(diff <= (position - j) * RUN, 0.0, NEG).astype(bf16)
            ka[j * RUN : (j + 1) * RUN, HEAD : 2 * HEAD] = mask
        scores = dot(ka[0:length, :], qt[...]) * SCALE2
        sbuf[0:length, :] = scores
        largest = jnp.max(scores.reshape(length // 8, 8, ROWS), axis=0)
        row_max = jnp.max(largest, axis=0, keepdims=True)
        weights = jnp.exp2(sbuf[0:length, :] - row_max).astype(bf16)
        wbuf[0:length, :] = weights
        mixed = dot_t0(va[0:length, 0:HEAD + TAIL], weights)
        inverse = 1.0 / mixed[HEAD : HEAD + 1, :]
        out_t = (mixed[0:HEAD, :] * inverse).astype(bf16)
        out_n = jnp.transpose(out_t)
        do_t = (jnp.transpose(don[...]).astype(f32) * inverse).astype(bf16)
        don[...] = jnp.transpose(do_t)
        delta = -jnp.sum(do_t.astype(f32) * out_t.astype(f32), axis=0, keepdims=True)
        high = delta.astype(bf16).astype(f32)
        middle = (delta - high).astype(bf16).astype(f32)
        low = delta - high - middle
        dot_t[0:HEAD, :] = do_t
        dot_t[HEAD : 2 * HEAD, :] = jnp.where(
            depth_of == 0,
            high,
            jnp.where(depth_of == 1, middle, jnp.where(depth_of == 2, low, 0.0)),
        ).astype(bf16)
        for h in range(HEADS):
            outs[rows, h * HEAD : (h + 1) * HEAD] = out_n[h * RUN : (h + 1) * RUN, :]
        weights = wbuf[0:length, :]
        dscore = weights * dot(va[0:length, :], dot_t[...]).astype(bf16)
        dva[0:length, :] += dot(weights, don[...])
        dka[0:length, :] += dot(dscore, qn[...])
        grad_n = jnp.transpose((dot_t0(ka[0:length, 0:HEAD], dscore) * SCALE).astype(bf16))
        for h in range(HEADS):
            gqs[rows, h * HEAD : (h + 1) * HEAD] = grad_n[h * RUN : (h + 1) * RUN, :]

    @pl.loop(0, 4)
    def _(a):
        position = ids_s[0, a]
        needed = (position + 1) * RUN
        line = pl.ds(pl.multiple_of(a % 2 * RUN, RUN), RUN)

        def take(q_ref, do_ref, base):
            for h in range(HEADS):
                columns = pl.ds(pl.multiple_of(base + h * HEAD, HEAD), HEAD)
                qn[h * RUN : (h + 1) * RUN, :] = q_ref[line, columns]
                don[h * RUN : (h + 1) * RUN, :] = do_ref[line, columns]

        @pl.when(a < 2)
        def _():
            take(q_refs[0], do_refs[0], core_ref[0] * width)

        @pl.when(a >= 2)
        def _():
            take(q_refs[1], do_refs[1], 0)

        for short, length in zip((0,) + LENGTHS, LENGTHS):

            @pl.when((needed > short) & (needed <= length))
            def _():
                run_block(a, position, length)

    copies = []
    for half in range(2):
        place = slice(half * TOK, (half + 1) * TOK)
        copies.append(pltpu.make_async_copy(outs.at[place], out_refs[half], out_sem.at[half]))
        copies.append(pltpu.make_async_copy(gqs.at[place], gq_refs[half], out_sem.at[2 + half]))
        copies[-2].start()
        copies[-1].start()
    for part in PART_ORDER:
        for unit in range(UNITS):
            for run in range(2):
                where = ids_s[part * SIDE + unit // 2, unit % 2 * 2 + run]
                place = pl.ds(pl.multiple_of(where * RUN, RUN), RUN)
                first = unit * TOK + run * RUN
                dkv[part, first : first + RUN, 0:HEAD] = (dka[place, :] * SCALE).astype(bf16)
                dkv[part, first : first + RUN, HEAD : 2 * HEAD] = dva[place, :].astype(bf16)
        copies.append(pltpu.make_async_copy(dkv.at[part], dkv_refs[part], dkv_sem.at[part]))
        copies[-1].start()
    for copy in copies:
        copy.wait()


PART_ORDER = (1, 2, 3, 0)


def attention(core, q, do, kv):
    local = pl.BlockSpec(memory_space=pltpu.VMEM)
    smem = pl.BlockSpec(memory_space=pltpu.SMEM)
    tokens = BLOCKS * RUN
    width = HEADS * HEAD
    wide = pltpu.HBM((TOK, width), bf16)
    part = pltpu.HBM((UNITS * TOK, 2 * HEAD), bf16)
    return pl.pallas_call(
        attention_kernel,
        out_shape=(wide,) * 4 + (part,) * SIDE,
        in_specs=[smem] + [local] * 8,
        out_specs=(pl.BlockSpec(memory_space=pltpu.HBM),) * 8,
        scratch_shapes=[
            pltpu.VMEM((SIDE * SIDE, HEAD), jnp.int32),
            pltpu.SMEM((SIDE * SIDE, HEAD), jnp.int32),
            pltpu.VMEM((2 * TOK, width), bf16),
            pltpu.VMEM((2 * TOK, width), bf16),
            pltpu.VMEM((SIDE, UNITS * TOK, 2 * HEAD), bf16),
            pltpu.VMEM((tokens, 2 * HEAD), bf16),
            pltpu.VMEM((tokens, 2 * HEAD), bf16),
            pltpu.VMEM((ROWS, HEAD), bf16),
            pltpu.VMEM((2 * HEAD, ROWS), bf16),
            pltpu.VMEM((ROWS, HEAD), bf16),
            pltpu.VMEM((2 * HEAD, ROWS), bf16),
            pltpu.VMEM((tokens, ROWS), f32),
            pltpu.VMEM((tokens, ROWS), bf16),
            pltpu.VMEM((tokens, HEAD), f32),
            pltpu.VMEM((tokens, HEAD), f32),
            pltpu.SemaphoreType.DMA,
            pltpu.SemaphoreType.DMA((4,)),
            pltpu.SemaphoreType.DMA((SIDE,)),
        ],
        compiler_params=pltpu.CompilerParams(vmem_limit_bytes=VLIMIT * 2**20),
        name="attention",
    )(core, *q, *do, *kv)


VLIMIT = 40


def unit_kernel(core_ref, where_hbm, keys_hbm, values_hbm, mine_ref, other_ref, where, keys, values, sem):
    copies = [
        pltpu.make_async_copy(where_hbm, where, sem.at[0]),
        pltpu.make_async_copy(keys_hbm, keys, sem.at[1]),
        pltpu.make_async_copy(values_hbm, values, sem.at[2]),
    ]
    for copy in copies:
        copy.start()
    for copy in copies:
        copy.wait()
    lane = lax.broadcasted_iota(jnp.int32, (TAIL, 2 * HEAD), 1)
    first, second = where[0] // RUN, where[RUN] // RUN

    def tail(base):
        ids = jnp.where(lane == base, first, jnp.where(lane == base + 1, second, 0))
        return ids.astype(f32).astype(bf16)

    mine_ref[TOK : TOK + TAIL, :] = tail(0)
    other_ref[TOK : TOK + TAIL, :] = tail(2)

    def fill(low_ref, high_ref):
        low_ref[0:TOK, 0:HEAD] = keys[:, 0:HEAD]
        low_ref[0:TOK, HEAD : 2 * HEAD] = values[:, 0:HEAD]
        high_ref[0:TOK, 0:HEAD] = keys[:, HEAD : 2 * HEAD]
        high_ref[0:TOK, HEAD : 2 * HEAD] = values[:, HEAD : 2 * HEAD]

    @pl.when(core_ref[0] == 0)
    def _():
        fill(mine_ref, other_ref)

    @pl.when(core_ref[0] != 0)
    def _():
        fill(other_ref, mine_ref)


def key_units(core, positions, keys, values):
    vmem = pl.BlockSpec(memory_space=pltpu.VMEM)
    hbm = pl.BlockSpec(memory_space=pltpu.HBM)
    unit = jax.ShapeDtypeStruct((TOK + TAIL, 2 * HEAD), bf16)
    return pl.pallas_call(
        unit_kernel,
        out_shape=(unit, unit),
        in_specs=[pl.BlockSpec(memory_space=pltpu.SMEM), hbm, hbm, hbm],
        out_specs=(vmem, vmem),
        scratch_shapes=[
            pltpu.SMEM((TOK,), jnp.int32),
            pltpu.VMEM((TOK, 2 * HEAD), bf16),
            pltpu.VMEM((TOK, 2 * HEAD), bf16),
            pltpu.SemaphoreType.DMA((3,)),
        ],
        compiler_params=pltpu.CompilerParams(vmem_limit_bytes=8 * 2**20),
        name="units",
    )(core, *(pltpu.with_memory_space_constraint(x, pltpu.HBM) for x in (positions, keys, values)))


def swap(x):
    return lax.ppermute(x, ("outer", "inner"), [(i, (i + 16) % 32) for i in range(32)])


def shift(x, stage, distance):
    pairs = []
    for core in range(2):
        for z in range(SIDE):
            for y in range(SIDE):
                if core == stage:
                    far = z * SIDE + (y + distance) % SIDE
                else:
                    far = (z + distance) % SIDE * SIDE + y
                pairs.append((core * 16 + z * SIDE + y, core * 16 + far))
    return lax.ppermute(x, ("outer", "inner"), pairs)


def body(queries, keys, values, output_cotangent, positions):
    core = lax.axis_index("outer")

    def pick(x, which):
        width = x.shape[1] // 2
        return lax.dynamic_slice_in_dim(x, which * width, width, axis=1)

    core_index = core.astype(jnp.int32).reshape(1)
    kv_mine, kv_other = key_units(core_index, positions, keys, values)
    kv_other = swap(kv_other)
    kv_own = jnp.concatenate([kv_mine[:TOK], kv_other[:TOK], kv_mine[TOK:] + kv_other[TOK:]], 0)
    line = [kv_own] + [shift(kv_own, 0, d) for d in ORDER]
    line = lax.optimization_barrier(tuple(line) + (queries, output_cotangent))
    queries, output_cotangent = line[4:]
    line = jnp.concatenate(line[:4], 0)
    lines = [line] + [shift(line, 1, d) for d in ORDER]
    q_other = swap(pick(queries, 1 - core))
    do_other = swap(pick(output_cotangent, 1 - core))

    results = attention(
        core_index,
        (queries, q_other),
        (output_cotangent, do_other),
        lines,
    )
    outs, grads, parts = results[:2], results[2:4], results[4:]

    def total(terms):
        return functools.reduce(jnp.add, [t.astype(f32) for t in terms]).astype(bf16)

    def cut(x, i):
        return x[i * 2 * TOK : (i + 1) * 2 * TOK]

    line = total([parts[0]] + [shift(parts[1 + i], 1, -d) for i, d in enumerate(ORDER)])
    dkv = total([cut(line, 0)] + [shift(cut(line, 1 + i), 0, -d) for i, d in enumerate(ORDER)])
    dkv_mine, dkv_other = dkv[:TOK], swap(dkv[TOK:])

    def join(mine, other):
        return jnp.where(
            core == 0, jnp.concatenate([mine, other], 1), jnp.concatenate([other, mine], 1)
        )

    attn_out = join(outs[0], swap(outs[1]))
    grad_queries = join(grads[0], swap(grads[1]))
    key_gradient = join(dkv_mine[:, :HEAD], dkv_other[:, :HEAD])
    value_gradient = join(dkv_mine[:, HEAD:], dkv_other[:, HEAD:])
    return attn_out, grad_queries, key_gradient, value_gradient


ORDER = (2, 1, 3)


def solution(mesh):
    tokens = ("outer", "inner")
    split = P(tokens, "head")
    return jax.shard_map(
        body,
        mesh=mesh,
        in_specs=(split, split, split, split, P(tokens)),
        out_specs=(split, split, split, split),
        check_vma=False,
    )
```

```python
import functools
import math

import jax
import jax.numpy as jnp
from jax import lax
from jax.experimental import pallas as pl
from jax.experimental.pallas import tpu as pltpu
from jax.sharding import PartitionSpec as P

HEAD = 128
HEADS = 8
RUN = 64
ROWS = RUN * HEADS
TOK = 128
TAIL = 16
SIDE = 4
UNITS = 2 * SIDE
BLOCKS = 64
CHUNK = 1024
LENGTHS = (1024, 2048, 2560, 3072, 3584, 4096)
SCALE = HEAD**-0.5
SCALE2 = SCALE * math.log2(math.e)
NEG = -1e30

bf16 = jnp.bfloat16
f32 = jnp.float32


def dot(a, b):
    return lax.dot_general(a, b, (((1,), (0,)), ((), ())), preferred_element_type=f32)


def dot_t0(a, b):
    return lax.dot_general(a, b, (((0,), (0,)), ((), ())), preferred_element_type=f32)


def attention_kernel(*refs):
    core_ref = refs[0]
    q_refs, do_refs = refs[1:3], refs[3:5]
    kv_refs = refs[5:9]
    out_refs, gq_refs = refs[9:11], refs[11:13]
    dkv_refs = refs[13:17]
    (ids_v, ids_s, outs, gqs, dkv, ka, va, qn, qt, don, dot_t, sbuf, wbuf) = refs[17:30]
    (dka, dva, ids_sem, out_sem, dkv_sem) = refs[30:]
    tokens = BLOCKS * RUN
    step = 2 * TOK + TAIL
    width = HEADS * HEAD

    for part in range(SIDE):
        for pair in range(SIDE):
            tail = kv_refs[part][pair * step + 2 * TOK : (pair + 1) * step, 0:HEAD]
            row = part * SIDE + pair
            ids_v[row : row + 1, :] = tail.astype(f32)[0:1, :].astype(jnp.int32)
    fetch = pltpu.make_async_copy(ids_v, ids_s, ids_sem)
    fetch.start()

    lane = lax.broadcasted_iota(jnp.int32, (RUN, HEAD), 1)
    sub = lax.broadcasted_iota(jnp.int32, (RUN, HEAD), 0)
    diff = jnp.where(lane < RUN, sub - lane, -(1 << 30))
    ones3 = jnp.where(lax.broadcasted_iota(jnp.int32, (CHUNK, HEAD), 1) < 3, 1.0, 0.0).astype(bf16)
    token_of = lax.broadcasted_iota(jnp.int32, (HEAD, ROWS), 1) & (RUN - 1)
    depth_of = lax.broadcasted_iota(jnp.int32, (HEAD, ROWS), 0)
    qt[HEAD : 2 * HEAD, :] = jnp.where(token_of == depth_of, 1.0, 0.0).astype(bf16)

    @pl.loop(0, tokens // CHUNK)
    def _(c):
        s = pl.ds(pl.multiple_of(c * CHUNK, CHUNK), CHUNK)
        va[s, HEAD : 2 * HEAD] = ones3
        dka[s, :] = jnp.zeros((CHUNK, HEAD), f32)
        dva[s, :] = jnp.zeros((CHUNK, HEAD), f32)

    fetch.wait()

    for part in range(SIDE):
        for unit in range(UNITS):
            for run in range(2):
                where = ids_s[part * SIDE + unit // 2, unit % 2 * 2 + run]
                place = pl.ds(pl.multiple_of(where * RUN, RUN), RUN)
                first = unit // 2 * step + unit % 2 * TOK + run * RUN
                ka[place, 0:HEAD] = kv_refs[part][first : first + RUN, 0:HEAD]
                va[place, 0:HEAD] = kv_refs[part][first : first + RUN, HEAD : 2 * HEAD]

    def run_block(a, position, length):
        rows = pl.ds(pl.multiple_of(a * RUN, RUN), RUN)
        qt[0:HEAD, :] = jnp.transpose(qn[...])
        for j in range(length // RUN):
            mask = jnp.where(diff <= (position - j) * RUN, 0.0, NEG).astype(bf16)
            ka[j * RUN : (j + 1) * RUN, HEAD : 2 * HEAD] = mask
        scores = dot(ka[0:length, :], qt[...]) * SCALE2
        sbuf[0:length, :] = scores
        largest = jnp.max(scores.reshape(length // 8, 8, ROWS), axis=0)
        row_max = jnp.max(largest, axis=0, keepdims=True)
        weights = jnp.exp2(sbuf[0:length, :] - row_max).astype(bf16)
        wbuf[0:length, :] = weights
        mixed = dot_t0(va[0:length, 0:HEAD + TAIL], weights)
        inverse = 1.0 / mixed[HEAD : HEAD + 1, :]
        out_t = (mixed[0:HEAD, :] * inverse).astype(bf16)
        out_n = jnp.transpose(out_t)
        do_t = (jnp.transpose(don[...]).astype(f32) * inverse).astype(bf16)
        don[...] = jnp.transpose(do_t)
        delta = -jnp.sum(do_t.astype(f32) * out_t.astype(f32), axis=0, keepdims=True)
        high = delta.astype(bf16).astype(f32)
        middle = (delta - high).astype(bf16).astype(f32)
        low = delta - high - middle
        dot_t[0:HEAD, :] = do_t
        dot_t[HEAD : 2 * HEAD, :] = jnp.where(
            depth_of == 0,
            high,
            jnp.where(depth_of == 1, middle, jnp.where(depth_of == 2, low, 0.0)),
        ).astype(bf16)
        for h in range(HEADS):
            outs[rows, h * HEAD : (h + 1) * HEAD] = out_n[h * RUN : (h + 1) * RUN, :]
        weights = wbuf[0:length, :]
        dscore = weights * dot(va[0:length, :], dot_t[...]).astype(bf16)
        dva[0:length, :] += dot(weights, don[...])
        dka[0:length, :] += dot(dscore, qn[...])
        grad_n = jnp.transpose((dot_t0(ka[0:length, 0:HEAD], dscore) * SCALE).astype(bf16))
        for h in range(HEADS):
            gqs[rows, h * HEAD : (h + 1) * HEAD] = grad_n[h * RUN : (h + 1) * RUN, :]

    def leaving(half):
        place = slice(half * TOK, (half + 1) * TOK)
        return [
            pltpu.make_async_copy(outs.at[place], out_refs[half], out_sem.at[half]),
            pltpu.make_async_copy(gqs.at[place], gq_refs[half], out_sem.at[2 + half]),
        ]

    @pl.loop(0, 4)
    def _(a):
        @pl.when(a == 2)
        def _():
            for copy in leaving(0):
                copy.start()

        position = ids_s[0, a]
        needed = (position + 1) * RUN
        line = pl.ds(pl.multiple_of(a % 2 * RUN, RUN), RUN)

        def take(q_ref, do_ref, base):
            for h in range(HEADS):
                columns = pl.ds(pl.multiple_of(base + h * HEAD, HEAD), HEAD)
                qn[h * RUN : (h + 1) * RUN, :] = q_ref[line, columns]
                don[h * RUN : (h + 1) * RUN, :] = do_ref[line, columns]

        @pl.when(a < 2)
        def _():
            take(q_refs[0], do_refs[0], core_ref[0] * width)

        @pl.when(a >= 2)
        def _():
            take(q_refs[1], do_refs[1], 0)

        for short, length in zip((0,) + LENGTHS, LENGTHS):

            @pl.when((needed > short) & (needed <= length))
            def _():
                run_block(a, position, length)

    for copy in leaving(1):
        copy.start()
    copies = leaving(0) + leaving(1)
    for part in PART_ORDER:
        for unit in range(UNITS):
            for run in range(2):
                where = ids_s[part * SIDE + unit // 2, unit % 2 * 2 + run]
                place = pl.ds(pl.multiple_of(where * RUN, RUN), RUN)
                first = unit * TOK + run * RUN
                dkv[part, first : first + RUN, 0:HEAD] = (dka[place, :] * SCALE).astype(bf16)
                dkv[part, first : first + RUN, HEAD : 2 * HEAD] = dva[place, :].astype(bf16)
        copies.append(pltpu.make_async_copy(dkv.at[part], dkv_refs[part], dkv_sem.at[part]))
        copies[-1].start()
    for copy in copies:
        copy.wait()


PART_ORDER = (1, 2, 3, 0)


def attention(core, q, do, kv):
    local = pl.BlockSpec(memory_space=pltpu.VMEM)
    smem = pl.BlockSpec(memory_space=pltpu.SMEM)
    tokens = BLOCKS * RUN
    width = HEADS * HEAD
    wide = pltpu.HBM((TOK, width), bf16)
    part = pltpu.HBM((UNITS * TOK, 2 * HEAD), bf16)
    return pl.pallas_call(
        attention_kernel,
        out_shape=(wide,) * 4 + (part,) * SIDE,
        in_specs=[smem] + [local] * 8,
        out_specs=(pl.BlockSpec(memory_space=pltpu.HBM),) * 8,
        scratch_shapes=[
            pltpu.VMEM((SIDE * SIDE, HEAD), jnp.int32),
            pltpu.SMEM((SIDE * SIDE, HEAD), jnp.int32),
            pltpu.VMEM((2 * TOK, width), bf16),
            pltpu.VMEM((2 * TOK, width), bf16),
            pltpu.VMEM((SIDE, UNITS * TOK, 2 * HEAD), bf16),
            pltpu.VMEM((tokens, 2 * HEAD), bf16),
            pltpu.VMEM((tokens, 2 * HEAD), bf16),
            pltpu.VMEM((ROWS, HEAD), bf16),
            pltpu.VMEM((2 * HEAD, ROWS), bf16),
            pltpu.VMEM((ROWS, HEAD), bf16),
            pltpu.VMEM((2 * HEAD, ROWS), bf16),
            pltpu.VMEM((tokens, ROWS), f32),
            pltpu.VMEM((tokens, ROWS), bf16),
            pltpu.VMEM((tokens, HEAD), f32),
            pltpu.VMEM((tokens, HEAD), f32),
            pltpu.SemaphoreType.DMA,
            pltpu.SemaphoreType.DMA((4,)),
            pltpu.SemaphoreType.DMA((SIDE,)),
        ],
        compiler_params=pltpu.CompilerParams(vmem_limit_bytes=VLIMIT * 2**20),
        name="attention",
    )(core, *q, *do, *kv)


VLIMIT = 40


def unit_kernel(core_ref, where_hbm, keys_hbm, values_hbm, mine_ref, other_ref, where, keys, values, sem):
    copies = [
        pltpu.make_async_copy(where_hbm, where, sem.at[0]),
        pltpu.make_async_copy(keys_hbm, keys, sem.at[1]),
        pltpu.make_async_copy(values_hbm, values, sem.at[2]),
    ]
    for copy in copies:
        copy.start()
    for copy in copies:
        copy.wait()
    lane = lax.broadcasted_iota(jnp.int32, (TAIL, 2 * HEAD), 1)
    first, second = where[0] // RUN, where[RUN] // RUN

    def tail(base):
        ids = jnp.where(lane == base, first, jnp.where(lane == base + 1, second, 0))
        return ids.astype(f32).astype(bf16)

    mine_ref[TOK : TOK + TAIL, :] = tail(0)
    other_ref[TOK : TOK + TAIL, :] = tail(2)

    def fill(low_ref, high_ref):
        low_ref[0:TOK, 0:HEAD] = keys[:, 0:HEAD]
        low_ref[0:TOK, HEAD : 2 * HEAD] = values[:, 0:HEAD]
        high_ref[0:TOK, 0:HEAD] = keys[:, HEAD : 2 * HEAD]
        high_ref[0:TOK, HEAD : 2 * HEAD] = values[:, HEAD : 2 * HEAD]

    @pl.when(core_ref[0] == 0)
    def _():
        fill(mine_ref, other_ref)

    @pl.when(core_ref[0] != 0)
    def _():
        fill(other_ref, mine_ref)


def key_units(core, positions, keys, values):
    vmem = pl.BlockSpec(memory_space=pltpu.VMEM)
    hbm = pl.BlockSpec(memory_space=pltpu.HBM)
    unit = jax.ShapeDtypeStruct((TOK + TAIL, 2 * HEAD), bf16)
    return pl.pallas_call(
        unit_kernel,
        out_shape=(unit, unit),
        in_specs=[pl.BlockSpec(memory_space=pltpu.SMEM), hbm, hbm, hbm],
        out_specs=(vmem, vmem),
        scratch_shapes=[
            pltpu.SMEM((TOK,), jnp.int32),
            pltpu.VMEM((TOK, 2 * HEAD), bf16),
            pltpu.VMEM((TOK, 2 * HEAD), bf16),
            pltpu.SemaphoreType.DMA((3,)),
        ],
        compiler_params=pltpu.CompilerParams(vmem_limit_bytes=8 * 2**20),
        name="units",
    )(core, *(pltpu.with_memory_space_constraint(x, pltpu.HBM) for x in (positions, keys, values)))


def swap(x):
    return lax.ppermute(x, ("outer", "inner"), [(i, (i + 16) % 32) for i in range(32)])


def shift(x, stage, distance):
    pairs = []
    for core in range(2):
        for z in range(SIDE):
            for y in range(SIDE):
                if core == stage:
                    far = z * SIDE + (y + distance) % SIDE
                else:
                    far = (z + distance) % SIDE * SIDE + y
                pairs.append((core * 16 + z * SIDE + y, core * 16 + far))
    return lax.ppermute(x, ("outer", "inner"), pairs)


def body(queries, keys, values, output_cotangent, positions):
    core = lax.axis_index("outer")

    def pick(x, which):
        width = x.shape[1] // 2
        return lax.dynamic_slice_in_dim(x, which * width, width, axis=1)

    core_index = core.astype(jnp.int32).reshape(1)
    kv_mine, kv_other = key_units(core_index, positions, keys, values)
    kv_other = swap(kv_other)
    kv_own = jnp.concatenate([kv_mine[:TOK], kv_other[:TOK], kv_mine[TOK:] + kv_other[TOK:]], 0)
    line = [kv_own] + [shift(kv_own, 0, d) for d in ORDER]
    line = lax.optimization_barrier(tuple(line) + (queries, output_cotangent))
    queries, output_cotangent = line[4:]
    line = jnp.concatenate(line[:4], 0)
    lines = [line] + [shift(line, 1, d) for d in ORDER]
    q_other = swap(pick(queries, 1 - core))
    do_other = swap(pick(output_cotangent, 1 - core))

    results = attention(
        core_index,
        (queries, q_other),
        (output_cotangent, do_other),
        lines,
    )
    outs, grads, parts = results[:2], results[2:4], results[4:]

    def total(terms):
        return functools.reduce(jnp.add, [t.astype(f32) for t in terms]).astype(bf16)

    def cut(x, i):
        return x[i * 2 * TOK : (i + 1) * 2 * TOK]

    line = total([parts[0]] + [shift(parts[1 + i], 1, -d) for i, d in enumerate(ORDER)])
    dkv = total([cut(line, 0)] + [shift(cut(line, 1 + i), 0, -d) for i, d in enumerate(ORDER)])
    dkv_mine, dkv_other = dkv[:TOK], swap(dkv[TOK:])

    def join(mine, other):
        return jnp.where(
            core == 0, jnp.concatenate([mine, other], 1), jnp.concatenate([other, mine], 1)
        )

    attn_out = join(outs[0], swap(outs[1]))
    grad_queries = join(grads[0], swap(grads[1]))
    key_gradient = join(dkv_mine[:, :HEAD], dkv_other[:, :HEAD])
    value_gradient = join(dkv_mine[:, HEAD:], dkv_other[:, HEAD:])
    return attn_out, grad_queries, key_gradient, value_gradient


ORDER = (2, 1, 3)


def solution(mesh):
    tokens = ("outer", "inner")
    split = P(tokens, "head")
    return jax.shard_map(
        body,
        mesh=mesh,
        in_specs=(split, split, split, split, P(tokens)),
        out_specs=(split, split, split, split),
        check_vma=False,
    )
```
